32 devices in a mesh: plane: 2 (over core), row: 4 (over z), col: 4 (over y, x).
Axes of the slice: x: 2, y: 2, z: 4, core: 2. Of those that a mesh axis runs over, the one named last changes fastest.
Arguments:
- velocity: float32 [3, 4, 4096, 4096], P(None, 'plane', 'row', 'col'), may hold values from -60 to 60
Outputs:
- dissipation: float32 [4, 4096, 4096], P('plane', 'row', 'col')
- fine_means: float32 [128, 128], P('row', 'col')
- coarse_means: float32 [4, 4], replicated
The draws below stay inside these ranges and needn't reach their ends.
All inputs are finite; a program needn't handle non-finite values.
Results may differ from the reference program's by a relative error of at most 0.000078.
Values sent between devices are 32-bit elements; how exact they have to be, the bound alone decides.
A program may use at most 320 MiB of HBM per device.

```python
import math
import jax
import jax.numpy as jnp

N = 4096
FINE = 32
COARSE = 1024
NZ = 4


def draw_velocity(key, part):
    base_key = jax.random.fold_in(key, 7)
    subkeys = jax.random.split(base_key, 4)
    full_shape = (3, NZ, N, N)
    noise_vals = jnp.clip(jax.random.normal(subkeys[0], full_shape, jnp.float32), -5.0, 5.0)
    row_scale = jnp.exp(jax.random.uniform(subkeys[1], (N,), jnp.float32, -1.15, 1.15))
    col_scale = jnp.exp(jax.random.uniform(subkeys[2], (N,), jnp.float32, -1.15, 1.15))
    plane_scale = jnp.exp(jax.random.uniform(subkeys[3], (NZ,), jnp.float32, -0.5, 0.5))
    position = jnp.arange(N).astype(jnp.float32) / N
    plane_pos = jnp.arange(NZ).astype(jnp.float32) / NZ
    rise_fac = jnp.exp(0.5 * math.log(3.0) * position)
    amplitude = 0.12 * (plane_scale * jnp.exp(0.55 * plane_pos))[:, None, None]
    amplitude = amplitude * (row_scale * rise_fac)[None, :, None] * (col_scale * rise_fac)[None, None, :]
    values = noise_vals * amplitude[None]
    return values


def setup_inputs(seed: int = 0) -> dict:
    seeds = jax.random.split(jax.random.key(seed), 2)
    return {
        "velocity": draw_velocity(jax.random.fold_in(seeds[1], 71), 0),
    }


def wave_numbers(length):
    indices = jnp.arange(length)
    signed = jnp.where(indices < length // 2, indices, indices - length)
    signed = jnp.where(indices == length // 2, 0, signed)
    return signed.astype(jnp.float32) * (2.0 * math.pi / length)


def derivative(values, along):
    length = values.shape[along]
    wavenum = wave_numbers(length)
    if along == 1:
        wavenum = wavenum.reshape(length, 1)
    spectrum = jnp.fft.fft(values, axis=along)
    return jnp.real(jnp.fft.ifft(spectrum * (1j * wavenum), axis=along)).astype(jnp.float32)


def z_diff(values):
    return (jnp.roll(values, -1, axis=0) - jnp.roll(values, 1, axis=0)) * 0.5


def box_means(dissip, edge):
    planes = dissip.shape[0]
    count = dissip.shape[1] // edge
    column_sum = jnp.sum(dissip, axis=0)
    boxed = column_sum.reshape(count, edge, count, edge).sum(axis=(1, 3))
    return boxed * (1.0 / (planes * edge * edge))


def reference(velocity):
    vel_u = velocity[0]
    vel_v = velocity[1]
    vel_w = velocity[2]
    single = derivative(vel_u, 1)
    dissip = single * single
    single = derivative(vel_v, 2)
    dissip = dissip + single * single
    single = z_diff(vel_w)
    dissip = dissip + single * single
    cross_sum = derivative(vel_u, 2) + derivative(vel_v, 1)
    dissip = dissip + 0.5 * cross_sum * cross_sum
    cross_sum = z_diff(vel_u) + derivative(vel_w, 1)
    dissip = dissip + 0.5 * cross_sum * cross_sum
    cross_sum = z_diff(vel_v) + derivative(vel_w, 2)
    dissip = dissip + 0.5 * cross_sum * cross_sum
    return dissip, box_means(dissip, FINE), box_means(dissip, COARSE)
```

```python
import math

import jax
import jax.numpy as jnp
from jax import lax
from jax.sharding import PartitionSpec as P

N = 4096
FINE = 32
COARSE = 1024
SPLITS = 2


precise = lax.Precision.HIGH


def with_halo(cells, sides, width):
    for axis, dim in sides:
        count = lax.axis_size(axis)
        head = lax.slice_in_dim(cells, 0, width, axis=dim)
        tail = lax.slice_in_dim(cells, cells.shape[dim] - width, cells.shape[dim], axis=dim)
        cells = jnp.concatenate(
            [
                lax.ppermute(tail, axis, [(i, (i + 1) % count) for i in range(count)]),
                cells,
                lax.ppermute(head, axis, [((i + 1) % count, i) for i in range(count)]),
            ],
            axis=dim,
        )
    return cells


def kernel_table(size, skew):
    i = lax.broadcasted_iota(jnp.int32, (size, size), 0)
    j = lax.broadcasted_iota(jnp.int32, (size, size), 1)
    shift = i - j
    sign = jnp.where(shift % 2 == 0, 1.0, -1.0)
    wrapped = jnp.where(shift > size // 2, shift - size, shift)
    wrapped = jnp.where(shift < -(size // 2), shift + size, wrapped)
    angle = wrapped.astype(jnp.float32) * (math.pi / size)
    safe = jnp.where(shift == 0, 1.0, angle)
    if skew:
        top = jnp.where(wrapped == shift, 1.0, -1.0)
    else:
        top = jnp.where(jnp.abs(shift) * 2 == size, 0.0, jnp.cos(safe))
    value = sign * (math.pi / size) * top / jnp.sin(safe)
    return jnp.where(shift == 0, 0.0, value)


def make_tables(length):
    tables = []
    size = length
    for _ in range(SPLITS):
        size //= 2
        tables.append(kernel_table(size, True))
    tables.append(kernel_table(size, False))
    return tables


def apply_table(table, values, dim):
    if dim == 1:
        return jnp.einsum("ij,zjm->zim", table, values, precision=precise)
    return jnp.einsum("zmj,ij->zmi", values, table, precision=precise)


def split_derivative(values, tables, dim, scale):
    if len(tables) == 1:
        return apply_table(tables[0], values, dim) * scale
    half = values.shape[dim] // 2
    low = lax.slice_in_dim(values, 0, half, axis=dim)
    high = lax.slice_in_dim(values, half, 2 * half, axis=dim)
    even = split_derivative(low + high, tables[1:], dim, scale * 0.5)
    odd = apply_table(tables[0], low - high, dim) * (scale * 0.5)
    return jnp.concatenate([even + odd, even - odd], axis=dim)


def take(values, index, size, dim):
    return lax.dynamic_slice_in_dim(values, index * size, size, axis=dim)


def send_out(field, axis, dim):
    count = lax.axis_size(axis)
    me = lax.axis_index(axis)
    other = 3 - dim
    size = field.shape[other] // count
    pieces = [None] * count
    pieces[0] = take(field, me, size, other)
    for step in (range(1, count)):
        block = take(field, (me + step) % count, size, other)
        moved = lax.ppermute(block, axis, [(i, (i + step) % count) for i in range(count)])
        pieces[count - step] = moved
    return jnp.concatenate(pieces, axis=dim)


def send_back(line, axis, dim):
    count = lax.axis_size(axis)
    me = lax.axis_index(axis)
    other = 3 - dim
    length = line.shape[dim] // count
    size = line.shape[other]
    shape = list(line.shape)
    shape[dim] = length
    shape[other] = size * count
    result = jnp.zeros(shape, line.dtype)
    for step in range(count):
        block = lax.slice_in_dim(line, step * length, (step + 1) * length, axis=dim)
        if step:
            block = lax.ppermute(block, axis, [(i, (i + step) % count) for i in range(count)])
        source = (me - step + count) % count
        result = lax.dynamic_update_slice_in_dim(result, block, source * size, axis=other)
    return result


def per_device(velocity):
    x_local = velocity.shape[2]
    y_local = velocity.shape[3]
    plane_count = velocity.shape[1] * lax.axis_size("plane")
    rows = lax.axis_size("row")
    cols = lax.axis_size("col")
    x_lines = [send_out(velocity[c], "row", 1) for c in range(3)]
    y_lines = [send_out(velocity[c], "col", 2) for c in range(3)]
    x_tables = make_tables(x_local * rows)
    y_tables = x_tables if x_local * rows == y_local * cols else make_tables(y_local * cols)
    grad_x = [send_back(split_derivative(x_lines[c], x_tables, 1, 1.0), "row", 1) for c in range(3)]
    grad_y = [send_back(split_derivative(y_lines[c], y_tables, 2, 1.0), "col", 2) for c in range(3)]
    padded = with_halo(velocity, (("plane", 1),), 1)
    grad_z = (padded[:, 2:] - padded[:, :-2]) * 0.5
    cross_xy = grad_y[0] + grad_x[1]
    cross_xz = grad_z[0] + grad_x[2]
    cross_yz = grad_z[1] + grad_y[2]
    dissip = grad_x[0] * grad_x[0] + grad_y[1] * grad_y[1] + grad_z[2] * grad_z[2]
    dissip = dissip + 0.5 * (cross_xy * cross_xy + cross_xz * cross_xz + cross_yz * cross_yz)
    column_sum = jnp.sum(dissip, axis=0)
    fine_local = column_sum.reshape(x_local // FINE, FINE, y_local // FINE, FINE).sum(axis=(1, 3))
    fine_total = lax.psum(fine_local, "plane")
    fine_means = fine_total * (1.0 / (plane_count * FINE * FINE))
    local_total = jnp.sum(fine_local)
    row_boxes = x_local * rows // COARSE
    col_boxes = y_local * cols // COARSE
    box_row = lax.axis_index("row") * x_local // COARSE
    box_col = lax.axis_index("col") * y_local // COARSE
    rows_hit = (lax.iota(jnp.int32, row_boxes) == box_row).astype(jnp.float32)
    cols_hit = (lax.iota(jnp.int32, col_boxes) == box_col).astype(jnp.float32)
    partial_map = rows_hit[:, None] * cols_hit[None, :] * local_total
    coarse_total = lax.psum(partial_map, ("plane", "row", "col"))
    coarse_means = coarse_total * (1.0 / (plane_count * COARSE * COARSE))
    return (dissip, fine_means, coarse_means)


def solution(mesh):
    in_specs = (P(None, "plane", "row", "col"),)
    out_specs = (P("plane", "row", "col"), P("row", "col"), P())
    return jax.shard_map(
        per_device, mesh=mesh, in_specs=in_specs, out_specs=out_specs, check_vma=False
    )
```
